256 devices in a mesh: row: 16 (over x_lo, z), col: 16 (over y, x_hi, core).
Axes of the slice: x: 4 (x_hi: 2, x_lo: 2; x = x_hi * 2 + x_lo), y: 4, z: 8, core: 2. Of those that a mesh axis runs over, the one named last changes fastest.
Arguments:
- upper_out: bfloat16 [2048, 6144], P('row', 'col'), may hold values from -6 to 6
- lower_out: bfloat16 [2048, 6144], P('row', 'col'), may hold values from -6 to 6
- upper_cot: bfloat16 [2048, 6144], P('row', 'col'), may hold values from -6 to 6
- lower_cot: bfloat16 [2048, 6144], P('row', 'col'), may hold values from -6 to 6
- w_expand: bfloat16 [6144, 24576], P('col', 'row'), may hold values from -0.078125 to 0.078125
- w_reduce: bfloat16 [24576, 6144], P('row', 'col'), may hold values from -0.0390625 to 0.0390625
Outputs:
- lower_input: bfloat16 [2048, 6144], P('row', 'col')
- upper_total: bfloat16 [2048, 6144], P('row', 'col')
- expand_grad: bfloat16 [6144, 24576], P('col', 'row')
- reduce_grad: bfloat16 [24576, 6144], P('row', 'col')
The draws below stay inside these ranges and needn't reach their ends.
All inputs are finite; a program needn't handle non-finite values.
Results may differ from the reference program's by a relative error of at most 0.023.
Values may be sent and summed in bfloat16 or wider, within the bound.
No kernel may reach another device: no remote copies, remote signals or barrier semaphores. Data moves between devices by JAX's collectives and lax.ppermute only.
A program may use at most 128 MiB of HBM per device.

```python
import math
import jax
import jax.numpy as jnp
from jax import lax

D = 6144
FF = 24576
TOKENS = 2048
N_ROW = 16
N_COL = 16


def block_levels(key, dims, split, least, high):
    level, own = 1.0, jax.random.fold_in(key, 6)
    for axis_at, blocks in split:
        steps = jnp.exp(jax.random.uniform(jax.random.fold_in(own, axis_at), (blocks,), jnp.float32, least / len(split), high / len(split)))
        level = level * jnp.repeat(steps, dims[axis_at] // blocks).reshape([-1 if axis == axis_at else 1 for axis in range(len(dims))])
    return level


def noise(own_key, shape, deviation, most, cuts=(), held_as=jnp.bfloat16):
    values = jax.random.normal(own_key, shape, jnp.float32) * deviation
    if len(cuts) > 0:
        values = block_levels(own_key, shape, cuts, -0.22, 0.18) * values
    return jnp.clip(values, min=-most, max=most).astype(held_as)


def setup_inputs(seed: int = 0) -> dict:
    key_list = jax.random.split(jax.random.key(seed), 7)
    upper_out = noise(key_list[0], (TOKENS, D), 1.0, 6.0, ((0, 16), (1, 16)))
    lower_out = noise(key_list[1], (TOKENS, D), 1.0, 6.0, ((0, 16), (1, 16)))
    upper_cot = noise(key_list[2], (TOKENS, D), 1.0, 6.0, ((0, 16), (1, 16)))
    lower_cot = noise(key_list[3], (TOKENS, D), 1.0, 6.0, ((0, 16), (1, 16)))
    w_expand = noise(key_list[4], (D, FF), D ** -0.5, 0.078125, ((0, 16), (1, 16)))
    w_reduce = noise(key_list[5], (FF, D), FF ** -0.5, 0.0390625, ((0, 16), (1, 16)))
    return dict(upper_out=upper_out, lower_out=lower_out, upper_cot=upper_cot, lower_cot=lower_cot, w_expand=w_expand, w_reduce=w_reduce)


root_half = 0.7071067811865476
inv_root_tau = 0.3989422804014327

def gelu_slope(pre):
    return 0.5 * (1.0 + lax.erf(pre * root_half)) + pre * jnp.exp(-0.5 * pre * pre) * inv_root_tau

def grouped_dot(left, right, groups):
    width = left.shape[1] // groups

    def advance(total, index):
        start = index * width
        piece = jnp.dot(lax.dynamic_slice_in_dim(left, start, width, 1), lax.dynamic_slice_in_dim(right, start, width, 0), preferred_element_type=jnp.float32)
        rounded = lax.optimization_barrier(piece.astype(jnp.bfloat16))
        return (total + rounded.astype(jnp.float32), None)
    initial = jnp.zeros((left.shape[0], right.shape[1]), jnp.float32)
    total, unused = lax.scan(advance, initial, jnp.arange(groups, dtype=jnp.int32))
    return total

def reference(upper_out, lower_out, upper_cot, lower_cot, w_expand, w_reduce):
    scale = 1.0 / math.sqrt(TOKENS)
    pre = grouped_dot(upper_out, w_expand, N_COL)
    acts = jax.nn.gelu(pre, approximate=False).astype(jnp.bfloat16)
    branch = grouped_dot(acts, w_reduce, N_ROW)
    lower_input = (lower_out.astype(jnp.float32) - branch).astype(jnp.bfloat16)
    reduce_grad = (jnp.dot(acts.T, lower_cot, preferred_element_type=jnp.float32) * scale).astype(jnp.bfloat16)
    back = grouped_dot(lower_cot, w_reduce.T, N_COL)
    slopes = (back * gelu_slope(pre)).astype(jnp.bfloat16)
    expand_grad = (jnp.dot(upper_out.T, slopes, preferred_element_type=jnp.float32) * scale).astype(jnp.bfloat16)
    carried = grouped_dot(slopes, w_expand.T, N_ROW)
    upper_total = (upper_cot.astype(jnp.float32) + carried).astype(jnp.bfloat16)
    return (lower_input, upper_total, expand_grad, reduce_grad)
```

```python
import math

import jax
import jax.numpy as jnp
import numpy as np
from jax import lax
from jax.sharding import Mesh, PartitionSpec as P

root_half = 0.7071067811865476
inv_root_tau = 0.3989422804014327
axes = ("xl", "z", "y", "xh", "core")
sizes = dict(xl=2, z=8, y=4, xh=2, core=2)
f32 = jnp.float32
bf16 = jnp.bfloat16


def gelu_slope(pre):
    return 0.5 * (1.0 + lax.erf(pre * root_half)) + pre * jnp.exp(-0.5 * pre * pre) * inv_root_tau


def move(value, names, steps):
    dims = tuple(sizes[name] for name in names)
    pairs = []
    for source in range(math.prod(dims)):
        at = np.unravel_index(source, dims)
        to = tuple((int(a) + s) % d for a, s, d in zip(at, steps, dims))
        pairs.append((source, int(np.ravel_multi_index(to, dims))))
    return lax.ppermute(value, names, pairs)


def to_quad(value, k):
    return move(value, ("xh", "core"), (k >> 1, k & 1))


def quad_weights(w, axis):
    across = move(w, ("xh",), (1,))
    beside = move(w, ("core",), (1,))
    diagonal = move(across, ("core",), (1,))
    return jnp.concatenate([w, beside, across, diagonal], axis=axis)


def ring_gather(chunk):
    ahead = behind = chunk
    out = [chunk]
    for step in range(1, 5):
        ahead = move(ahead, ("z",), (1,))
        out.append(ahead)
        if step < 4:
            behind = move(behind, ("z",), (-1,))
            out.append(behind)
    return out


slot_of = {0: 0, -1: 1, 1: 2, -2: 3, 2: 4, -3: 5, 3: 6, 4: 7}


def ring_scatter(partial):
    parts = partial.reshape(8, 64, partial.shape[1])

    def part(offset):
        return parts[slot_of[offset]]

    ahead = move(part(4), ("z",), (1,))
    behind = move(part(-3), ("z",), (-1,))
    for step in (3, 2, 1):
        if step < 3:
            behind = move((behind.astype(f32) + part(-step).astype(f32)).astype(bf16), ("z",), (-1,))
        ahead = move((ahead.astype(f32) + part(step).astype(f32)).astype(bf16), ("z",), (1,))
    return ahead.astype(f32) + behind.astype(f32) + part(0).astype(f32)


def y_scatter(partial, y):
    parts = partial.reshape(4, 128, partial.shape[1])
    got = [move(lax.dynamic_index_in_dim(parts, (y + k) % 4, 0, False), ("y",), (k,)) for k in (2, 1, 3)]
    total = lax.dynamic_index_in_dim(parts, y, 0, False).astype(f32)
    for piece in got:
        total = total + piece.astype(f32)
    return total


def y_gather(chunk, y):
    got = [(k, move(chunk, ("y",), (k,))) for k in (2, 1, 3)]
    whole = jnp.zeros((4,) + chunk.shape, chunk.dtype)
    whole = lax.dynamic_update_index_in_dim(whole, chunk, y, 0)
    for k, piece in got:
        whole = lax.dynamic_update_index_in_dim(whole, piece, (y + 4 - k) % 4, 0)
    return whole.reshape(512, chunk.shape[1])


def leave(partial, q):
    rows = ring_scatter(partial)
    other = move(rows[32:].astype(bf16), ("xl",), (1,))
    mine = (rows[:32] + other.astype(f32)).astype(bf16)
    blocks = [mine[:, k * 384 : (k + 1) * 384] for k in range(4)]
    whole = jnp.zeros((4, 32, 384), bf16)
    for k in range(4):
        piece = blocks[0] if k == 0 else to_quad(blocks[k], k)
        whole = lax.dynamic_update_index_in_dim(whole, piece, q ^ k, 0)
    return whole.reshape(128, 384).astype(f32)


def quad_scatter(block, scale, axis):
    sent = block((1, 3)).astype(bf16)
    kept = block((0, 2))
    got = move(sent, ("core",), (1,))
    both = kept.astype(f32) + got.astype(f32)
    own, far = jnp.split(both, 2, axis=axis)
    last = move(far.astype(bf16), ("xh",), (1,))
    return ((own + last.astype(f32)) * scale).astype(bf16)


def body(upper_out, lower_out, upper_cot, lower_cot, w_expand, w_reduce):
    scale = 1.0 / math.sqrt(2048.0)
    y = lax.axis_index("y")
    q = 2 * lax.axis_index("xh") + lax.axis_index("core")

    both = jnp.stack([upper_out, lower_cot]).reshape(2, 4, 32, 384)
    pieces = [lax.dynamic_index_in_dim(both, q ^ k, 1, False) for k in range(4)]
    pieces = [pieces[0]] + [to_quad(pieces[k], k) for k in (1, 2, 3)]
    own = jnp.concatenate(pieces, axis=2)
    far = move(own, ("xl",), (1,))
    start = jnp.concatenate([own, far], axis=1)

    we = quad_weights(w_expand, 0)
    wr = quad_weights(w_reduce, 1)
    upper = jnp.concatenate(ring_gather(start[0]), axis=0)
    cot = jnp.concatenate(ring_gather(start[1]), axis=0)

    pre_part = jnp.dot(upper, we, preferred_element_type=f32).astype(bf16)
    pre = y_scatter(pre_part, y)
    back_part = lax.dot_general(
        cot, wr, (((1,), (1,)), ((), ())), preferred_element_type=f32
    ).astype(bf16)
    back = y_scatter(back_part, y)
    acts = y_gather(jax.nn.gelu(pre, approximate=False).astype(bf16), y)
    slopes = y_gather((back * gelu_slope(pre)).astype(bf16), y)

    branch = leave(jnp.dot(acts, wr, preferred_element_type=f32).astype(bf16), q)
    lower_input = (lower_out.astype(f32) - branch).astype(bf16)

    def reduce_block(ks):
        side = jnp.concatenate([cot[:, k * 384 : (k + 1) * 384] for k in ks], axis=1)
        return lax.dot_general(acts, side, (((0,), (0,)), ((), ())), preferred_element_type=f32)

    reduce_grad = quad_scatter(reduce_block, scale, 1)

    carried_part = lax.dot_general(
        slopes, we, (((1,), (1,)), ((), ())), preferred_element_type=f32
    ).astype(bf16)
    carried = leave(carried_part, q)
    upper_total = (upper_cot.astype(f32) + carried).astype(bf16)

    def expand_block(ks):
        side = jnp.concatenate([upper[:, k * 384 : (k + 1) * 384] for k in ks], axis=1)
        return lax.dot_general(side, slopes, (((0,), (0,)), ((), ())), preferred_element_type=f32)

    expand_grad = quad_scatter(expand_block, scale, 0)
    return (lower_input, upper_total, expand_grad, reduce_grad)


def solution(mesh):
    fine = Mesh(mesh.devices.reshape(tuple(sizes[name] for name in axes)), axes)
    row, col = ("xl", "z"), ("y", "xh", "core")
    return jax.shard_map(
        body,
        mesh=fine,
        in_specs=(P(row, col), P(row, col), P(row, col), P(row, col), P(col, row), P(row, col)),
        out_specs=(P(row, col), P(row, col), P(col, row), P(row, col)),
        check_vma=False,
    )
```

```python
import math

import jax
import jax.numpy as jnp
import numpy as np
from jax import lax
from jax.experimental import pallas as pl
from jax.experimental.pallas import tpu as pltpu
from jax.sharding import Mesh, PartitionSpec as P

root_half = 0.7071067811865476
inv_root_tau = 0.3989422804014327
axes = ("xl", "z", "y", "xh", "core")
sizes = dict(xl=2, z=8, y=4, xh=2, core=2)
f32 = jnp.float32
bf16 = jnp.bfloat16
offsets = (0, -1, 1, -2, 2, -3, 3, 4)
flips = (3, 2, 1, 0)
heights = ((0, 128), (128, 256), (256, 320), (320, 384), (384, 512))
tile = 512


def gelu_slope(pre):
    return 0.5 * (1.0 + lax.erf(pre * root_half)) + pre * jnp.exp(-0.5 * pre * pre) * inv_root_tau


def move(value, names, steps):
    dims = tuple(sizes[name] for name in names)
    pairs = []
    for source in range(math.prod(dims)):
        at = np.unravel_index(source, dims)
        to = tuple((int(a) + s) % d for a, s, d in zip(at, steps, dims))
        pairs.append((source, int(np.ravel_multi_index(to, dims))))
    return lax.ppermute(value, names, pairs)


def together(*values):
    return lax.optimization_barrier(values)


def ring_gather(chunk, second):
    ahead = behind = chunk
    found = {0: chunk}
    for step in range(1, 5):
        ahead = move(ahead, ("z",), (1,))
        if step < 4:
            behind = move(behind, ("z",), (-1,))
            if step == 2:
                ahead, behind, second = together(ahead, behind, second)
            else:
                ahead, behind = together(ahead, behind)
            found[step] = behind
        found[-step if step < 4 else 4] = ahead
    return found, second


def add(*values):
    return sum((value.astype(f32) for value in values[1:]), values[0].astype(f32))


def ring_scatter(pieces, riders):
    part = dict(zip(offsets, pieces))
    ahead, behind = move(part[4], ("z",), (1,)), move(part[-3], ("z",), (-1,))
    ahead, behind, *riders = together(ahead, behind, *riders)
    rode = []
    for step in (3, 2, 1):
        sent = [add(ahead, part[step]).astype(bf16), riders[3 - step]]
        if step > 1:
            sent.append(add(behind, part[1 - step]).astype(bf16))
        sent = together(*sent)
        got = [move(sent[0], ("z",), (1,)), move(sent[1], ("xh",), (1,))]
        if step > 1:
            got.append(move(sent[2], ("z",), (-1,)))
        got = together(*got)
        ahead = got[0]
        if step > 1:
            behind = got[2]
        rode.append(got[1])
    return add(ahead, behind, part[0]), rode


def y_scatter(parts):
    got = [move(parts[k], ("y",), (k,)) for k in (2, 1, 3)]
    return sum((piece.astype(f32) for piece in got), parts[0].astype(f32))


def y_gather(chunk):
    last, following = together(move(chunk, ("y",), (1,)), move(chunk, ("y",), (-1,)))
    top, bottom = move(last[:64], ("y",), (1,)), move(following[64:], ("y",), (-1,))
    return [chunk, following, top, bottom, last]


def enter(values):
    n = values.shape[0]
    sent = jnp.broadcast_to(values.reshape(n, 1, 4, 32, 384).transpose(1, 2, 0, 3, 4), (2, 4, n, 32, 384))
    got = lax.all_to_all(sent.reshape(8, n, 32, 384), ("xl", "xh", "core"), 0, 0, tiled=True)
    return got.reshape(2, 4, n, 32, 384).transpose(2, 0, 3, 1, 4).reshape(n, 64, 1536)


def leave(rows):
    n = rows.shape[0]
    sent = rows.astype(bf16).reshape(n, 2, 32, 4, 384).transpose(1, 3, 0, 2, 4).reshape(8, n, 32, 384)
    got = lax.all_to_all(sent, ("xl", "xh", "core"), 0, 0, tiled=True)
    got = got.reshape(2, 4, n, 32, 384).astype(f32)
    return (got[0] + got[1]).transpose(1, 0, 2, 3).reshape(n, 128, 384)


def chunk_row(slot, y):
    return lax.rem(slot // 2 - y + 4, 4) * 128 + slot % 2 * 64


def feature(q, flip):
    return pl.multiple_of((q ^ flip) * 384, 128)


def run_kernel(kernel, where, inputs, in_specs, outputs, out_specs, scratch, transcendentals=0):
    spec = pltpu.PrefetchScalarGridSpec(
        num_scalar_prefetch=1, grid=(3,), in_specs=in_specs, out_specs=out_specs, scratch_shapes=scratch
    )
    return pl.pallas_call(
        kernel,
        grid_spec=spec,
        out_shape=outputs,
        compiler_params=pltpu.CompilerParams(vmem_limit_bytes=32 << 20),
        cost_estimate=pl.CostEstimate(
            flops=2 * 512 * 1536 * 1536, bytes_accessed=9 << 20, transcendentals=transcendentals
        ),
    )(where, *inputs)


def whole(shape):
    return pl.BlockSpec(shape, lambda t, where: (0, 0))


def part_kernel(from_pieces, transposed):
    count = 8 if from_pieces else 1

    def kernel(where, *refs):
        sources, weights = refs[:count], refs[count : count + 4]
        outs, ordered = refs[count + 4 : count + 8], refs[count + 8]
        q, y, z = where[0], where[1], where[2]

        @pl.when(pl.program_id(0) == 0)
        def _():
            for slot, offset in enumerate(offsets):
                row = pl.ds(pl.multiple_of(chunk_row(slot, y), 64), 64)
                for at, flip in enumerate(flips):
                    columns = pl.ds(feature(q, flip), 384)
                    if from_pieces:
                        block = sources[slot][:, columns]
                    else:
                        place = pl.multiple_of(lax.rem(z + 8 + offset, 8) * 64, 64)
                        block = sources[0][pl.ds(place, 64), columns]
                    ordered[row, at * 384 : (at + 1) * 384] = block

        axis = 1 if transposed else 0
        joined = jnp.concatenate([weights[k][...] for k in flips], axis=axis)
        product = lax.dot_general(
            ordered[...], joined, (((1,), (axis,)), ((), ())), preferred_element_type=f32
        ).astype(bf16)
        for k in range(4):
            outs[k][...] = product[k * 128 : (k + 1) * 128]

    def call(where, sources, weights):
        if transposed:
            weight_spec = pl.BlockSpec((tile, 384), lambda t, where: (t, 0))
        else:
            weight_spec = pl.BlockSpec((384, tile), lambda t, where: (0, t))
        source_shape = (64, 1536) if from_pieces else (512, 1536)
        results = run_kernel(
            kernel,
            where,
            (*sources, *weights),
            [whole(source_shape)] * count + [weight_spec] * 4,
            [jax.ShapeDtypeStruct((128, 1536), bf16)] * 4 + [jax.ShapeDtypeStruct((512, 1536), bf16)],
            [pl.BlockSpec((128, tile), lambda t, where: (0, t))] * 4 + [whole((512, 1536))],
            [],
        )
        return results[:4], results[4]

    return call


def back_kernel(to_pieces, transposed):
    count = 8 if to_pieces else 1

    def kernel(where, *refs):
        chunks, weights = refs[:5], refs[5:9]
        outs, joined, held = refs[9 : 9 + count], refs[9 + count], refs[10 + count]
        q, y, z = where[0], where[1], where[2]
        step = pl.program_id(0)

        @pl.when(step == 0)
        def _():
            for chunk, (low, high) in zip(chunks, heights):
                joined[low:high, :] = chunk[...]

        axis = 0 if transposed else 1
        side = jnp.concatenate([weights[k][...] for k in range(4)], axis=axis)
        held[...] = lax.dot_general(
            joined[...], side, (((1,), (1 - axis,)), ((), ())), preferred_element_type=f32
        ).astype(bf16)
        for slot, offset in enumerate(offsets):
            row = pl.ds(pl.multiple_of(chunk_row(slot, y), 64), 64)
            for k in range(4):
                columns = pl.ds(pl.multiple_of(feature(q, k) + step * 128, 128), 128)
                block = held[row, k * 128 : (k + 1) * 128]
                if to_pieces:
                    outs[slot][:, columns] = block
                else:
                    place = pl.multiple_of(lax.rem(z + 8 + offset, 8) * 64, 64)
                    outs[0][pl.ds(place, 64), columns] = block

    def call(where, chunks, weights):
        if transposed:
            weight_spec = pl.BlockSpec((128, 1536), lambda t, where: (t, 0))
        else:
            weight_spec = pl.BlockSpec((1536, 128), lambda t, where: (0, t))
        out_shape = (64, 1536) if to_pieces else (512, 1536)
        results = run_kernel(
            kernel,
            where,
            (*chunks, *weights),
            [whole((high - low, 1536)) for low, high in heights] + [weight_spec] * 4,
            [jax.ShapeDtypeStruct(out_shape, bf16)] * count + [jax.ShapeDtypeStruct((512, 1536), bf16)],
            [whole(out_shape)] * count + [whole((512, 1536))],
            [pltpu.VMEM((512, tile), bf16)],
        )
        return results[:count], results[count]

    return call


def quad_send(block):
    got_far = move(block(0).astype(bf16), ("core",), (1,))
    got = move(block(2).astype(bf16), ("core",), (1,))
    return (block(1) + got_far.astype(f32)).astype(bf16), block(3) + got.astype(f32)


def transposed_dot(left, right):
    return lax.dot_general(left, right, (((0,), (0,)), ((), ())), preferred_element_type=f32)


def body(upper_out, lower_out, upper_cot, lower_cot, w_expand, w_reduce):
    scale = 1.0 / math.sqrt(2048.0)
    q = 2 * lax.axis_index("xh") + lax.axis_index("core")
    where = jnp.stack([q, lax.axis_index("y"), lax.axis_index("z")]).astype(jnp.int32)

    start = enter(jnp.stack([upper_out, lower_cot]))
    start, w_expand = together(start, w_expand)
    expand_far = move(w_expand, ("xh",), (1,))
    expand_near = move(w_expand, ("core",), (1,))

    found, cot = ring_gather(start[0], start[1])
    cot = lax.all_gather(cot, "z", axis=0, tiled=True)
    found[4], expand_far, w_reduce = together(found[4], expand_far, w_reduce)
    expand_last = move(expand_far, ("core",), (1,))
    reduce_far = move(w_reduce, ("xh",), (1,))
    reduce_near = move(w_reduce, ("core",), (1,))

    expand_all = [w_expand, expand_near, expand_far, expand_last]
    pre_parts, upper = part_kernel(True, False)(where, [found[offset] for offset in offsets], expand_all)
    pre = y_scatter(pre_parts)
    act_own = jax.nn.gelu(pre, approximate=False).astype(bf16)
    act_own, reduce_far = together(act_own, reduce_far)
    reduce_last = move(reduce_far, ("core",), (1,))
    acts = y_gather(act_own)

    reduce_all = [w_reduce, reduce_near, reduce_far, reduce_last]
    back_parts, cot = part_kernel(False, True)(where, [cot], reduce_all)
    back = y_scatter(back_parts)
    slopes = y_gather((back * gelu_slope(pre)).astype(bf16))

    branch_parts, acts = back_kernel(False, False)(where, acts, reduce_all)
    branch = lax.psum_scatter(branch_parts[0], "z", scatter_dimension=0, tiled=True)
    far, own = quad_send(lambda at: transposed_dot(acts, cot[:, at * 384 : (at + 1) * 384]))
    last = move(far, ("xh",), (1,))
    slopes[2], last = together(slopes[2], last)
    reduce_grad = ((own + last.astype(f32)) * scale).astype(bf16)

    carried_parts, slopes = back_kernel(True, True)(where, slopes, expand_all)
    far, own = quad_send(lambda at: transposed_dot(upper[:, at * 384 : (at + 1) * 384], slopes))
    rows = [slice(at * 128, (at + 1) * 128) for at in range(3)]
    carried, last = ring_scatter(carried_parts, [far[part] for part in rows])
    expand_grad = jnp.concatenate(
        [((own[part] + piece.astype(f32)) * scale).astype(bf16) for part, piece in zip(rows, last)]
    )

    left = leave(jnp.stack([branch, carried.astype(bf16)]))
    lower_input = (lower_out.astype(f32) - left[0]).astype(bf16)
    upper_total = (upper_cot.astype(f32) + left[1]).astype(bf16)
    return (lower_input, upper_total, expand_grad, reduce_grad)


def solution(mesh):
    fine = Mesh(mesh.devices.reshape(tuple(sizes[name] for name in axes)), axes)
    row, col = ("xl", "z"), ("y", "xh", "core")
    return jax.shard_map(
        body,
        mesh=fine,
        in_specs=(P(row, col), P(row, col), P(row, col), P(row, col), P(col, row), P(row, col)),
        out_specs=(P(row, col), P(row, col), P(col, row), P(row, col)),
        check_vma=False,
    )
```

```python
import math

import jax
import jax.numpy as jnp
import numpy as np
from jax import lax
from jax.experimental import pallas as pl
from jax.experimental.pallas import tpu as pltpu
from jax.sharding import Mesh, PartitionSpec as P

root_half = 0.7071067811865476
inv_root_tau = 0.3989422804014327
axes = ("xl", "z", "y", "xh", "core")
sizes = dict(xl=2, z=8, y=4, xh=2, core=2)
f32 = jnp.float32
bf16 = jnp.bfloat16
offsets = (0, -1, 1, -2, 2, -3, 3, 4)
flips = (3, 2, 1, 0)
tile = 512


def gelu_slope(pre):
    return 0.5 * (1.0 + lax.erf(pre * root_half)) + pre * jnp.exp(-0.5 * pre * pre) * inv_root_tau


def move(value, names, steps):
    dims = tuple(sizes[name] for name in names)
    pairs = []
    for source in range(math.prod(dims)):
        at = np.unravel_index(source, dims)
        to = tuple((int(a) + s) % d for a, s, d in zip(at, steps, dims))
        pairs.append((source, int(np.ravel_multi_index(to, dims))))
    return lax.ppermute(value, names, pairs)


def together(*values):
    return lax.optimization_barrier(values)


def add(*values):
    return sum((value.astype(f32) for value in values[1:]), values[0].astype(f32))


def enter(values):
    n = values.shape[0]
    sent = jnp.broadcast_to(values.reshape(n, 1, 4, 32, 384).transpose(1, 2, 0, 3, 4), (2, 4, n, 32, 384))
    got = lax.all_to_all(sent.reshape(8, n, 32, 384), ("xl", "xh", "core"), 0, 0, tiled=True)
    return got.reshape(2, 4, n, 32, 384).transpose(2, 0, 3, 1, 4).reshape(n, 64, 1536)


def leave(rows):
    n = rows.shape[0]
    sent = rows.astype(bf16).reshape(n, 2, 32, 4, 384).transpose(1, 3, 0, 2, 4).reshape(8, n, 32, 384)
    got = lax.all_to_all(sent, ("xl", "xh", "core"), 0, 0, tiled=True)
    got = got.reshape(2, 4, n, 32, 384).astype(f32)
    return (got[0] + got[1]).transpose(1, 0, 2, 3).reshape(n, 128, 384)


def chunk_row(slot, y):
    return lax.rem(slot // 2 - y + 4, 4) * 128 + slot % 2 * 64


def feature(q, flip):
    return pl.multiple_of((q ^ flip) * 384, 128)


def y_move(value, k):
    return move(value, ("y",), (k,))


def quad_move(value, k):
    return move(value, ("xh", "core"), (k >> 1, k & 1))


def thirds(size):
    return [slice(at * size // 3, (at + 1) * size // 3) for at in range(3)]


def z_move(value, k):
    return move(value, ("z",), (k,))


def run_kernel(kernel, where, inputs, in_specs, outputs, out_specs, scratch, products=1):
    spec = pltpu.PrefetchScalarGridSpec(
        num_scalar_prefetch=1, grid=(3,), in_specs=in_specs, out_specs=out_specs, scratch_shapes=scratch
    )
    return pl.pallas_call(
        kernel,
        grid_spec=spec,
        out_shape=outputs,
        compiler_params=pltpu.CompilerParams(vmem_limit_bytes=(8 + 8 * products) << 20),
        cost_estimate=pl.CostEstimate(
            flops=products * 2 * 512 * 1536 * 1536, bytes_accessed=9 << 20, transcendentals=0
        ),
    )(where, *inputs)


def whole(shape):
    return pl.BlockSpec(shape, lambda t, where: (0,) * len(shape), pipeline_mode=pl.Buffered(1))


def whole_out(shape):
    return pl.BlockSpec(shape, lambda t, where: (0,) * len(shape))


def transposed_dot(left, right):
    return lax.dot_general(left, right, (((0,), (0,)), ((), ())), preferred_element_type=f32)


def part_kernel(where, pieces, weights, which):
    def kernel(where, *refs):
        sources, weights, outs, ordered = refs[:8], refs[8:12], refs[12:16], refs[16]
        q, y = where[0], where[1]

        @pl.when(pl.program_id(0) == 0)
        def _():
            for slot in range(8):
                row = pl.ds(pl.multiple_of(chunk_row(slot, y), 64), 64)
                for at, flip in enumerate(flips):
                    columns = pl.ds(feature(q, flip), 384)
                    ordered[row, at * 384 : (at + 1) * 384] = sources[slot][:, columns]

        joined = jnp.concatenate([weights[k][...] for k in flips], axis=which)
        product = lax.dot_general(
            ordered[...], joined, (((1,), (which,)), ((), ())), preferred_element_type=f32
        ).astype(bf16)
        for k in range(4):
            outs[k][...] = product[k * 128 : (k + 1) * 128]

    if which:
        weight_spec = pl.BlockSpec((tile, 384), lambda t, where: (t, 0))
    else:
        weight_spec = pl.BlockSpec((384, tile), lambda t, where: (0, t))
    results = run_kernel(
        kernel,
        where,
        (*pieces, *weights),
        [whole((64, 1536))] * 8 + [weight_spec] * 4,
        [jax.ShapeDtypeStruct((128, 1536), bf16)] * 4 + [jax.ShapeDtypeStruct((512, 1536), bf16)],
        [pl.BlockSpec((128, tile), lambda t, where: (0, t))] * 4 + [whole_out((512, 1536))],
        [],
    )
    return results[:4], results[4]


def join(chunks, joined):
    at = 0
    for chunk in chunks:
        joined[at : at + chunk.shape[0], :] = chunk[...]
        at += chunk.shape[0]


def spread(held, outs, q, y, step):
    for slot in range(8):
        row = pl.ds(pl.multiple_of(chunk_row(slot, y), 64), 64)
        for k in range(4):
            columns = pl.ds(pl.multiple_of(feature(q, k) + step * 128, 128), 128)
            outs[slot][:, columns] = held[row, k * 128 : (k + 1) * 128]


def branch_kernel(where, chunks, weights, cot):
    def kernel(where, *refs):
        chunks, weights, cot = refs[:4], refs[4:8], refs[8]
        outs, blocks, joined, held = refs[9:17], refs[17:21], refs[21], refs[22]
        q, y = where[0], where[1]
        step = pl.program_id(0)

        @pl.when(step == 0)
        def _():
            join(chunks, joined)

        side = jnp.concatenate([weights[k][...] for k in range(4)], axis=1)
        held[...] = jnp.dot(joined[...], side, preferred_element_type=f32).astype(bf16)
        spread(held, outs, q, y, step)
        units = pl.ds(pl.multiple_of(step * tile, tile), tile)
        product = transposed_dot(joined[:, units], cot[...]).astype(bf16)
        for at in range(4):
            blocks[at][...] = product[:, at * 384 : (at + 1) * 384]

    results = run_kernel(
        kernel,
        where,
        (*chunks, *weights, cot),
        [whole(chunk.shape) for chunk in chunks]
        + [pl.BlockSpec((1536, 128), lambda t, where: (0, t))] * 4
        + [whole((512, 1536))],
        [jax.ShapeDtypeStruct((64, 1536), bf16)] * 8 + [jax.ShapeDtypeStruct((1536, 384), bf16)] * 4,
        [whole_out((64, 1536))] * 8 + [pl.BlockSpec((tile, 384), lambda t, where: (t, 0))] * 4,
        [pltpu.VMEM((512, 1536), bf16), pltpu.VMEM((512, tile), bf16)],
        products=2,
    )
    return results[:8], results[8:]


def carried_kernel(where, joined, weights):
    def kernel(where, *refs):
        joined, weights, outs, held = refs[0], refs[1:5], refs[5:13], refs[13]
        q, y = where[0], where[1]
        step = pl.program_id(0)
        side = jnp.concatenate([weights[k][...] for k in range(4)], axis=0)
        held[...] = lax.dot_general(
            joined[...], side, (((1,), (1,)), ((), ())), preferred_element_type=f32
        ).astype(bf16)
        spread(held, outs, q, y, step)

    return run_kernel(
        kernel,
        where,
        (joined, *weights),
        [whole((512, 1536))] + [pl.BlockSpec((128, 1536), lambda t, where: (t, 0))] * 4,
        [jax.ShapeDtypeStruct((64, 1536), bf16)] * 8,
        [whole_out((64, 1536))] * 8,
        [pltpu.VMEM((512, tile), bf16)],
    )


def expand_kernel(where, upper, chunks, first):
    count = len(chunks)

    def kernel(where, *refs):
        upper, chunks, blocks = refs[0], refs[1 : 1 + count], refs[1 + count : 3 + count]
        step = pl.program_id(0)
        slopes = chunks[0]
        if count > 1:
            slopes = refs[3 + count]

            @pl.when(step == 0)
            def _():
                join(chunks, slopes)

        columns = [pl.ds(pl.multiple_of((first + at) * 384 + step * 128, 128), 128) for at in range(2)]
        left = jnp.concatenate([upper[:, column] for column in columns], axis=1)
        product = transposed_dot(left, slopes[...]).astype(bf16)
        for at in range(2):
            blocks[at][...] = product[at * 128 : (at + 1) * 128]

    return run_kernel(
        kernel,
        where,
        (upper, *chunks),
        [whole((512, 1536))] + [whole(chunk.shape) for chunk in chunks],
        [jax.ShapeDtypeStruct((384, 1536), bf16)] * 2
        + [jax.ShapeDtypeStruct((512, 1536), bf16)] * (count > 1),
        [pl.BlockSpec((128, 1536), lambda t, where: (t, 0))] * 2 + [whole_out((512, 1536))] * (count > 1),
        [],
    )


def body(upper_out, lower_out, upper_cot, lower_cot, w_expand, w_reduce):
    scale = 1.0 / math.sqrt(2048.0)
    q = 2 * lax.axis_index("xh") + lax.axis_index("core")
    where = jnp.stack([q, lax.axis_index("y"), lax.axis_index("z")]).astype(jnp.int32)

    start = enter(jnp.stack([upper_out, lower_cot]))
    start, w_expand, where = together(start, w_expand, where)
    expand_far = move(w_expand, ("xh",), (1,))
    expand_near = move(w_expand, ("core",), (1,))

    upper, cot = {0: start[0]}, {0: start[1]}
    upper[-1], upper[1], expand_near = together(z_move(upper[0], 1), z_move(upper[0], -1), expand_near)
    upper[-2], upper[2] = together(z_move(upper[-1], 1), z_move(upper[1], -1))
    upper[-3], upper[3], expand_far, w_reduce = together(
        z_move(upper[-2], 1), z_move(upper[2], -1), expand_far, w_reduce
    )
    reduce_far = quad_move(w_reduce, 2)
    upper[4], expand_last, reduce_near, cot[0] = together(
        z_move(upper[-3], 1), quad_move(expand_far, 1), quad_move(w_reduce, 1), cot[0]
    )
    expand_all = [w_expand, expand_near, expand_far, expand_last]
    pre_parts, upper = part_kernel(where, [upper[offset] for offset in offsets], expand_all, 0)
    cot[-1], cot[1], *pre_parts = together(z_move(cot[0], 1), z_move(cot[0], -1), *pre_parts)
    pre_one, pre_three, cot[-2], cot[2], pre_two = together(
        y_move(pre_parts[1], 1), y_move(pre_parts[3], 3), z_move(cot[-1], 1), z_move(cot[1], -1), pre_parts[2]
    )
    pre_two, cot[-3], cot[3], reduce_far = together(
        y_move(pre_two, 2), z_move(cot[-2], 1), z_move(cot[2], -1), reduce_far
    )
    pre = add(pre_parts[0], pre_one, pre_two, pre_three)
    act_own = jax.nn.gelu(pre, approximate=False).astype(bf16)

    act_own, reduce_far = together(act_own, reduce_far)
    acts = [y_move(act_own, k) for k in (3, 1, 2)]
    cot[4], reduce_last = together(z_move(cot[-3], 1), quad_move(reduce_far, 1))
    reduce_all = [w_reduce, reduce_near, reduce_far, reduce_last]
    back_parts, cot = part_kernel(where, [cot[offset] for offset in offsets], reduce_all, 1)
    following, last, opposite, *back_parts = together(*acts, *back_parts)

    branch, blocks = branch_kernel(where, [act_own, following, opposite, last], reduce_all, cot)
    branch = dict(zip(offsets, branch))
    back_one, back_three, back_two, branch[4], branch[-3], *blocks = together(
        *(y_move(back_parts[k], k) for k in (1, 3, 2)), branch[4], branch[-3], *blocks
    )
    back = add(back_parts[0], back_one, back_two, back_three)
    slope_own = (back * gelu_slope(pre)).astype(bf16)

    slope_own, blocks[0], ahead, behind = together(slope_own, blocks[0], branch[4], branch[-3])
    following, last, ahead, behind, got_far = together(
        y_move(slope_own, 3), y_move(slope_own, 1), z_move(ahead, 1), z_move(behind, -1), quad_move(blocks[0], 1)
    )
    ahead, behind = add(ahead, branch[3]).astype(bf16), add(behind, branch[-2]).astype(bf16)
    far = [add(blocks[1][rows], got_far[rows]).astype(bf16) for rows in thirds(1536)]
    ahead, behind, *far = together(ahead, behind, *far)
    top, bottom, ahead, behind, far[0] = together(
        y_move(last[:64], 1), y_move(following[64:], 3), z_move(ahead, 1), z_move(behind, -1), quad_move(far[0], 2)
    )
    ahead, behind = add(ahead, branch[2]).astype(bf16), add(behind, branch[-1]).astype(bf16)
    ahead, behind, far[1], top = together(ahead, behind, far[1], top)

    first, second, slopes = expand_kernel(where, upper, [slope_own, following, top, bottom, last], 0)
    carried = carried_kernel(where, slopes, expand_all)
    ahead, behind, far[1], got_far, *carried = together(
        z_move(ahead, 1), z_move(behind, -1), quad_move(far[1], 2), quad_move(first, 1), *carried
    )
    carried = dict(zip(offsets, carried))
    ahead = add(ahead, branch[1]).astype(bf16)
    riders = [far[2]] + [add(second[rows], got_far[rows]).astype(bf16) for rows in thirds(384)]

    carried_ahead, carried_behind, ahead, *riders = together(carried[4], carried[-3], ahead, *riders)
    carried_ahead, carried_behind, ahead, riders[0] = together(
        z_move(carried_ahead, 1), z_move(carried_behind, -1), z_move(ahead, 1), quad_move(riders[0], 2)
    )
    branch = add(ahead, behind, branch[0]).astype(bf16)
    for step in (3, 2):
        carried_ahead = add(carried_ahead, carried[step]).astype(bf16)
        carried_behind = add(carried_behind, carried[1 - step]).astype(bf16)
        carried_ahead, carried_behind, riders[4 - step], slopes = together(
            carried_ahead, carried_behind, riders[4 - step], slopes
        )
        if step == 3:
            inside = [quad_move(blocks[2], 1)]
        else:
            inside = expand_kernel(where, upper, [slopes], 2)
        carried_ahead, carried_behind, riders[4 - step], *inside = together(
            z_move(carried_ahead, 1), z_move(carried_behind, -1), quad_move(riders[4 - step], 2), *inside
        )
        if step == 3:
            reduce_got = inside[0]
    third, fourth = inside
    carried_ahead = add(carried_ahead, carried[1]).astype(bf16)
    carried_ahead, riders[3], third = together(carried_ahead, riders[3], third)
    carried_ahead, riders[3], got = together(
        z_move(carried_ahead, 1), quad_move(riders[3], 2), quad_move(third, 1)
    )
    far[2] = riders.pop(0)
    left = leave(jnp.stack([branch, add(carried_ahead, carried_behind, carried[0]).astype(bf16)]))
    lower_input = (lower_out.astype(f32) - left[0]).astype(bf16)
    upper_total = (upper_cot.astype(f32) + left[1]).astype(bf16)

    reduce_grad = jnp.concatenate(
        [
            (add(blocks[3][rows], reduce_got[rows], piece) * scale).astype(bf16)
            for rows, piece in zip(thirds(1536), far)
        ]
    )
    expand_grad = jnp.concatenate(
        [(add(fourth[rows], got[rows], piece) * scale).astype(bf16) for rows, piece in zip(thirds(384), riders)]
    )
    return (lower_input, upper_total, expand_grad, reduce_grad)


def solution(mesh):
    fine = Mesh(mesh.devices.reshape(tuple(sizes[name] for name in axes)), axes)
    row, col = ("xl", "z"), ("y", "xh", "core")
    return jax.shard_map(
        body,
        mesh=fine,
        in_specs=(P(row, col), P(row, col), P(row, col), P(row, col), P(col, row), P(row, col)),
        out_specs=(P(row, col), P(row, col), P(col, row), P(row, col)),
        check_vma=False,
    )
```

```python
import math

import jax
import jax.numpy as jnp
import numpy as np
from jax import lax
from jax.experimental import pallas as pl
from jax.experimental.pallas import tpu as pltpu
from jax.sharding import Mesh, PartitionSpec as P

root_half = 0.7071067811865476
inv_root_tau = 0.3989422804014327
axes = ("xl", "z", "y", "xh", "core")
sizes = dict(xl=2, z=8, y=4, xh=2, core=2)
f32 = jnp.float32
bf16 = jnp.bfloat16
offsets = (0, -1, 1, -2, 2, -3, 3, 4)
flips = (3, 2, 1, 0)
tile = 512


def gelu_slope(pre):
    return 0.5 * (1.0 + lax.erf(pre * root_half)) + pre * jnp.exp(-0.5 * pre * pre) * inv_root_tau


def move(value, names, steps):
    dims = tuple(sizes[name] for name in names)
    pairs = []
    for source in range(math.prod(dims)):
        at = np.unravel_index(source, dims)
        to = tuple((int(a) + s) % d for a, s, d in zip(at, steps, dims))
        pairs.append((source, int(np.ravel_multi_index(to, dims))))
    return lax.ppermute(value, names, pairs)


def together(*values):
    return lax.optimization_barrier(values)


def add(*values):
    return sum((value.astype(f32) for value in values[1:]), values[0].astype(f32))


def enter(values):
    n = values.shape[0]
    sent = jnp.broadcast_to(values.reshape(n, 1, 4, 32, 384).transpose(1, 2, 0, 3, 4), (2, 4, n, 32, 384))
    got = lax.all_to_all(sent.reshape(8, n, 32, 384), ("xl", "xh", "core"), 0, 0, tiled=True)
    return got.reshape(2, 4, n, 32, 384).transpose(2, 0, 3, 1, 4).reshape(n, 64, 1536)


def leave(rows):
    n = rows.shape[0]
    sent = rows.astype(bf16).reshape(n, 2, 32, 4, 384).transpose(1, 3, 0, 2, 4).reshape(8, n, 32, 384)
    got = lax.all_to_all(sent, ("xl", "xh", "core"), 0, 0, tiled=True)
    got = got.reshape(2, 4, n, 32, 384).astype(f32)
    return (got[0] + got[1]).transpose(1, 0, 2, 3).reshape(n, 128, 384)


def chunk_row(slot, y):
    return lax.rem(slot // 2 - y + 4, 4) * 128 + slot % 2 * 64


def feature(q, flip):
    return pl.multiple_of((q ^ flip) * 384, 128)


def y_move(value, k):
    return move(value, ("y",), (k,))


def quad_move(value, k):
    return move(value, ("xh", "core"), (k >> 1, k & 1))


def thirds(size):
    return [slice(at * size // 3, (at + 1) * size // 3) for at in range(3)]


def halves(size):
    return [slice(0, size // 2), slice(size // 2, size)]


def z_move(value, k):
    return move(value, ("z",), (k,))


def run_kernel(kernel, where, inputs, in_specs, outputs, out_specs, scratch, products=1, aliases=None):
    spec = pltpu.PrefetchScalarGridSpec(
        num_scalar_prefetch=1, grid=(3,), in_specs=in_specs, out_specs=out_specs, scratch_shapes=scratch
    )
    return pl.pallas_call(
        kernel,
        grid_spec=spec,
        out_shape=outputs,
        input_output_aliases=aliases or {},
        compiler_params=pltpu.CompilerParams(vmem_limit_bytes=(8 + 8 * products) << 20),
        cost_estimate=pl.CostEstimate(
            flops=products * 2 * 512 * 1536 * 1536, bytes_accessed=9 << 20, transcendentals=0
        ),
    )(where, *inputs)


def whole(shape):
    return pl.BlockSpec(shape, lambda t, where: (0,) * len(shape), pipeline_mode=pl.Buffered(1))


def whole_out(shape):
    return pl.BlockSpec(shape, lambda t, where: (0,) * len(shape))


def half_spec(which):
    return pl.BlockSpec((None, 64, 1536), lambda t, where: (which, 0, 0))


def transposed_dot(left, right):
    return lax.dot_general(left, right, (((0,), (0,)), ((), ())), preferred_element_type=f32)


def part_kernel(where, pieces, weights, which):
    def kernel(where, *refs):
        sources, weights, outs, ordered = refs[:8], refs[8:12], refs[12:16], refs[16]
        q, y = where[0], where[1]

        @pl.when(pl.program_id(0) == 0)
        def _():
            for slot in range(8):
                row = pl.ds(pl.multiple_of(chunk_row(slot, y), 64), 64)
                for at, flip in enumerate(flips):
                    columns = pl.ds(feature(q, flip), 384)
                    ordered[row, at * 384 : (at + 1) * 384] = sources[slot][:, columns]

        joined = jnp.concatenate([weights[k][...] for k in flips], axis=which)
        product = lax.dot_general(
            ordered[...], joined, (((1,), (which,)), ((), ())), preferred_element_type=f32
        ).astype(bf16)
        for k in range(4):
            outs[k][...] = product[k * 128 : (k + 1) * 128]

    if which:
        weight_spec = pl.BlockSpec((tile, 384), lambda t, where: (t, 0))
    else:
        weight_spec = pl.BlockSpec((384, tile), lambda t, where: (0, t))
    results = run_kernel(
        kernel,
        where,
        (*pieces, *weights),
        [whole((64, 1536))] * 8 + [weight_spec] * 4,
        [jax.ShapeDtypeStruct((128, 1536), bf16)] * 4 + [jax.ShapeDtypeStruct((512, 1536), bf16)],
        [pl.BlockSpec((128, tile), lambda t, where: (0, t))] * 4 + [whole_out((512, 1536))],
        [],
    )
    return results[:4], results[4]


def join(chunks, joined):
    at = 0
    for chunk in chunks:
        joined[at : at + chunk.shape[0], :] = chunk[...]
        at += chunk.shape[0]


def spread(held, outs, q, y, step):
    for slot in range(8):
        row = pl.ds(pl.multiple_of(chunk_row(slot, y), 64), 64)
        for k in range(4):
            columns = pl.ds(pl.multiple_of(feature(q, k) + step * 128, 128), 128)
            outs[slot][:, columns] = held[row, k * 128 : (k + 1) * 128]


def branch_kernel(where, chunks, weights, cot):
    def kernel(where, *refs):
        chunks, weights, cot = refs[:5], refs[5:9], refs[9]
        outs, blocks, joined, held = refs[10:18], refs[18:22], refs[22], refs[23]
        q, y = where[0], where[1]
        step = pl.program_id(0)

        @pl.when(step == 0)
        def _():
            join(chunks, joined)

        side = jnp.concatenate([weights[k][...] for k in range(4)], axis=1)
        held[...] = jnp.dot(joined[...], side, preferred_element_type=f32).astype(bf16)
        spread(held, outs, q, y, step)
        units = pl.ds(pl.multiple_of(step * tile, tile), tile)
        product = transposed_dot(joined[:, units], cot[...]).astype(bf16)
        for at in range(4):
            blocks[at][...] = product[:, at * 384 : (at + 1) * 384]

    results = run_kernel(
        kernel,
        where,
        (*chunks, *weights, cot),
        [whole(chunk.shape) for chunk in chunks]
        + [pl.BlockSpec((1536, 128), lambda t, where: (0, t))] * 4
        + [whole((512, 1536))],
        [jax.ShapeDtypeStruct((2, 64, 1536), bf16)] * 8 + [jax.ShapeDtypeStruct((1536, 384), bf16)] * 4,
        [half_spec(0)] * 8 + [pl.BlockSpec((tile, 384), lambda t, where: (t, 0))] * 4,
        [pltpu.VMEM((512, 1536), bf16), pltpu.VMEM((512, tile), bf16)],
        products=2,
    )
    return results[:8], results[8:]


def carried_kernel(where, chunks, weights, pairs):
    def kernel(where, *refs):
        chunks, weights, outs, joined, held = refs[:5], refs[5:9], refs[17:25], refs[25], refs[26]
        q, y = where[0], where[1]
        step = pl.program_id(0)

        @pl.when(step == 0)
        def _():
            join(chunks, joined)

        side = jnp.concatenate([weights[k][...] for k in range(4)], axis=0)
        held[...] = lax.dot_general(
            joined[...], side, (((1,), (1,)), ((), ())), preferred_element_type=f32
        ).astype(bf16)
        spread(held, outs, q, y, step)

    results = run_kernel(
        kernel,
        where,
        (*chunks, *weights, *pairs),
        [whole(chunk.shape) for chunk in chunks]
        + [pl.BlockSpec((128, 1536), lambda t, where: (t, 0))] * 4
        + [pl.BlockSpec(memory_space=pl.ANY)] * 8,
        [jax.ShapeDtypeStruct((2, 64, 1536), bf16)] * 8 + [jax.ShapeDtypeStruct((512, 1536), bf16)],
        [half_spec(1)] * 8 + [whole_out((512, 1536))],
        [pltpu.VMEM((512, tile), bf16)],
        aliases={10 + slot: slot for slot in range(8)},
    )
    return results[:8], results[8]


def expand_kernel(where, upper, slopes):
    def kernel(where, upper, slopes, *blocks):
        step = pl.program_id(0)
        columns = [pl.ds(pl.multiple_of(at * 384 + step * 128, 128), 128) for at in range(4)]
        left = jnp.concatenate([upper[:, column] for column in columns], axis=1)
        product = transposed_dot(left, slopes[...]).astype(bf16)
        for at in range(4):
            blocks[at][...] = product[at * 128 : (at + 1) * 128]

    return run_kernel(
        kernel,
        where,
        (upper, slopes),
        [whole((512, 1536))] * 2,
        [jax.ShapeDtypeStruct((384, 1536), bf16)] * 4,
        [pl.BlockSpec((128, 1536), lambda t, where: (t, 0))] * 4,
        [],
    )


def body(upper_out, lower_out, upper_cot, lower_cot, w_expand, w_reduce):
    scale = 1.0 / math.sqrt(2048.0)
    q = 2 * lax.axis_index("xh") + lax.axis_index("core")
    where = jnp.stack([q, lax.axis_index("y"), lax.axis_index("z")]).astype(jnp.int32)

    start = enter(jnp.stack([upper_out, lower_cot]))
    start, w_expand, where = together(start, w_expand, where)
    expand_far = move(w_expand, ("xh",), (1,))
    expand_near = move(w_expand, ("core",), (1,))

    upper, cot = {0: start[0]}, {0: start[1]}
    upper[-1], upper[1], expand_near = together(z_move(upper[0], 1), z_move(upper[0], -1), expand_near)
    upper[-2], upper[2] = together(z_move(upper[-1], 1), z_move(upper[1], -1))
    upper[-3], upper[3], cot[-1], cot[1], expand_far, w_reduce = together(
        z_move(upper[-2], 1), z_move(upper[2], -1), z_move(cot[0], 1), z_move(cot[0], -1), expand_far, w_reduce
    )
    reduce_far = quad_move(w_reduce, 2)
    upper[4], expand_last, reduce_near, cot[-1], cot[1] = together(
        z_move(upper[-3], 1), quad_move(expand_far, 1), quad_move(w_reduce, 1), cot[-1], cot[1]
    )
    expand_all = [w_expand, expand_near, expand_far, expand_last]
    pre_parts, upper = part_kernel(where, [upper[offset] for offset in offsets], expand_all, 0)
    cot[-2], cot[2], *pre_parts = together(z_move(cot[-1], 1), z_move(cot[1], -1), *pre_parts)
    pre_one, pre_three, cot[-3], cot[3], pre_two = together(
        y_move(pre_parts[1], 1), y_move(pre_parts[3], 3), z_move(cot[-2], 1), z_move(cot[2], -1), pre_parts[2]
    )
    pre_two, cot[4], reduce_far = together(y_move(pre_two, 2), z_move(cot[-3], 1), reduce_far)
    pre = add(pre_parts[0], pre_one, pre_two, pre_three)
    act_own = jax.nn.gelu(pre, approximate=False).astype(bf16)

    act_own, reduce_far = together(act_own, reduce_far)
    last, following = y_move(act_own, 1), y_move(act_own, 3)
    reduce_all = [w_reduce, reduce_near, reduce_far, quad_move(reduce_far, 1)]
    back_parts, cot = part_kernel(where, [cot[offset] for offset in offsets], reduce_all, 1)
    last, following, *back_parts = together(last, following, *back_parts)
    top, bottom, back_one, back_three, back_two = together(
        y_move(last[:64], 1), y_move(following[64:], 3), y_move(back_parts[1], 1), y_move(back_parts[3], 3), back_parts[2]
    )

    pairs, blocks = branch_kernel(where, [act_own, following, top, bottom, last], reduce_all, cot)
    back_two, *blocks = together(y_move(back_two, 2), *blocks)
    back = add(back_parts[0], back_one, back_two, back_three)
    slope_own = (back * gelu_slope(pre)).astype(bf16)

    slope_own, blocks[0], blocks[2] = together(slope_own, blocks[0], blocks[2])
    following, last, got_far, reduce_got = together(
        y_move(slope_own, 3), y_move(slope_own, 1), quad_move(blocks[0], 1), quad_move(blocks[2], 1)
    )
    far = [add(blocks[1][rows], got_far[rows]).astype(bf16) for rows in thirds(1536)]
    top, bottom, *far = together(last[:64], following[64:], *far)
    top, bottom, far[0] = together(y_move(top, 1), y_move(bottom, 3), quad_move(far[0], 2))

    pairs, slopes = carried_kernel(where, [slope_own, following, top, bottom, last], expand_all, pairs)
    part = dict(zip(offsets, pairs))

    ahead, behind, far[1] = together(part[4][0], part[4][1], far[1])
    ahead, behind, far[1], *more = together(
        z_move(ahead, 1), z_move(behind, -1), quad_move(far[1], 2), *expand_kernel(where, upper, slopes)
    )
    ahead = jnp.stack([add(ahead, part[3][0]).astype(bf16), part[3][1]])
    behind = jnp.stack([part[-3][0], add(behind, part[-3][1]).astype(bf16)])
    ahead, behind, far[2], more[0] = together(ahead, behind, far[2], more[0])
    ahead, behind, far[2], got_far = together(
        z_move(ahead, 1), z_move(behind, -1), quad_move(far[2], 2), quad_move(more[0], 1)
    )
    riders = [add(more[1][rows], got_far[rows]).astype(bf16) for rows in halves(384)]
    for step in (2, 1):
        ahead = add(ahead, part[step]).astype(bf16)
        behind = add(behind, part[-step]).astype(bf16)
        ahead, behind, riders[2 - step] = together(ahead, behind, riders[2 - step])
        inside = [quad_move(more[2], 1)] if step == 2 else []
        ahead, behind, riders[2 - step], *inside = together(
            z_move(ahead, 1), z_move(behind, -1), quad_move(riders[2 - step], 2), *inside
        )
        if step == 2:
            got = inside[0]
    left = leave(add(ahead, behind, part[0]).astype(bf16))
    lower_input = (lower_out.astype(f32) - left[0]).astype(bf16)
    upper_total = (upper_cot.astype(f32) + left[1]).astype(bf16)

    reduce_grad = jnp.concatenate(
        [
            (add(blocks[3][rows], reduce_got[rows], piece) * scale).astype(bf16)
            for rows, piece in zip(thirds(1536), far)
        ]
    )
    expand_grad = jnp.concatenate(
        [(add(more[3][rows], got[rows], piece) * scale).astype(bf16) for rows, piece in zip(halves(384), riders)]
    )
    return (lower_input, upper_total, expand_grad, reduce_grad)


def solution(mesh):
    fine = Mesh(mesh.devices.reshape(tuple(sizes[name] for name in axes)), axes)
    row, col = ("xl", "z"), ("y", "xh", "core")
    return jax.shard_map(
        body,
        mesh=fine,
        in_specs=(P(row, col), P(row, col), P(row, col), P(row, col), P(col, row), P(row, col)),
        out_specs=(P(row, col), P(row, col), P(col, row), P(row, col)),
        check_vma=False,
    )
```

```python
import math

import jax
import jax.numpy as jnp
import numpy as np
from jax import lax
from jax.experimental import pallas as pl
from jax.experimental.pallas import tpu as pltpu
from jax.sharding import Mesh, PartitionSpec as P

root_half = 0.7071067811865476
inv_root_tau = 0.3989422804014327
axes = ("xl", "z", "y", "xh", "core")
sizes = dict(xl=2, z=8, y=4, xh=2, core=2)
f32 = jnp.float32
bf16 = jnp.bfloat16
offsets = (0, -1, 1, -2, 2, -3, 3, 4)
flips = (3, 2, 1, 0)
tile = 512


def gelu_slope(pre):
    return 0.5 * (1.0 + lax.erf(pre * root_half)) + pre * jnp.exp(-0.5 * pre * pre) * inv_root_tau


def move(value, names, steps):
    dims = tuple(sizes[name] for name in names)
    pairs = []
    for source in range(math.prod(dims)):
        at = np.unravel_index(source, dims)
        to = tuple((int(a) + s) % d for a, s, d in zip(at, steps, dims))
        pairs.append((source, int(np.ravel_multi_index(to, dims))))
    return lax.ppermute(value, names, pairs)


def together(*values):
    return lax.optimization_barrier(values)


def add(*values):
    return sum((value.astype(f32) for value in values[1:]), values[0].astype(f32))


def enter(values):
    n = values.shape[0]
    sent = jnp.broadcast_to(values.reshape(n, 1, 4, 32, 384).transpose(1, 2, 0, 3, 4), (2, 4, n, 32, 384))
    got = lax.all_to_all(sent.reshape(8, n, 32, 384), ("xl", "xh", "core"), 0, 0, tiled=True)
    return got.reshape(2, 4, n, 32, 384).transpose(2, 0, 3, 1, 4).reshape(n, 64, 1536)


def leave(rows):
    n = rows.shape[0]
    sent = rows.astype(bf16).reshape(n, 2, 32, 4, 384).transpose(1, 3, 0, 2, 4).reshape(8, n, 32, 384)
    got = lax.all_to_all(sent, ("xl", "xh", "core"), 0, 0, tiled=True)
    got = got.reshape(2, 4, n, 32, 384).astype(f32)
    return (got[0] + got[1]).transpose(1, 0, 2, 3).reshape(n, 128, 384)


def chunk_row(slot, y):
    return lax.rem(slot // 2 - y + 4, 4) * 128 + slot % 2 * 64


def feature(q, flip):
    return pl.multiple_of((q ^ flip) * 384, 128)


def y_move(value, k):
    return move(value, ("y",), (k,))


def quad_move(value, k):
    return move(value, ("xh", "core"), (k >> 1, k & 1))


def thirds(size):
    return [slice(at * size // 3, (at + 1) * size // 3) for at in range(3)]


def halves(size):
    return [slice(0, size // 2), slice(size // 2, size)]


def z_move(value, k):
    return move(value, ("z",), (k,))


def run_kernel(kernel, where, inputs, in_specs, outputs, out_specs, scratch, products=1, aliases=None):
    spec = pltpu.PrefetchScalarGridSpec(
        num_scalar_prefetch=1, grid=(3,), in_specs=in_specs, out_specs=out_specs, scratch_shapes=scratch
    )
    return pl.pallas_call(
        kernel,
        grid_spec=spec,
        out_shape=outputs,
        input_output_aliases=aliases or {},
        compiler_params=pltpu.CompilerParams(vmem_limit_bytes=(8 + 8 * products) << 20),
        cost_estimate=pl.CostEstimate(
            flops=products * 2 * 512 * 1536 * 1536, bytes_accessed=9 << 20, transcendentals=0
        ),
    )(where, *inputs)


def whole(shape):
    return pl.BlockSpec(shape, lambda t, where: (0,) * len(shape), pipeline_mode=pl.Buffered(1))


def whole_out(shape):
    return pl.BlockSpec(shape, lambda t, where: (0,) * len(shape))


def half_spec(which):
    return pl.BlockSpec((None, 64, 1536), lambda t, where: (which, 0, 0))


def transposed_dot(left, right):
    return lax.dot_general(left, right, (((0,), (0,)), ((), ())), preferred_element_type=f32)


def part_kernel(where, pieces, weights, which):
    def kernel(where, *refs):
        sources, weights, outs, ordered = refs[:8], refs[8:12], refs[12:16], refs[16]
        q, y = where[0], where[1]

        @pl.when(pl.program_id(0) == 0)
        def _():
            for slot in range(8):
                row = pl.ds(pl.multiple_of(chunk_row(slot, y), 64), 64)
                for at, flip in enumerate(flips):
                    columns = pl.ds(feature(q, flip), 384)
                    ordered[row, at * 384 : (at + 1) * 384] = sources[slot][:, columns]

        joined = jnp.concatenate([weights[k][...] for k in flips], axis=which)
        product = lax.dot_general(
            ordered[...], joined, (((1,), (which,)), ((), ())), preferred_element_type=f32
        ).astype(bf16)
        for k in range(4):
            outs[k][...] = product[k * 128 : (k + 1) * 128]

    if which:
        weight_spec = pl.BlockSpec((tile, 384), lambda t, where: (t, 0))
    else:
        weight_spec = pl.BlockSpec((384, tile), lambda t, where: (0, t))
    results = run_kernel(
        kernel,
        where,
        (*pieces, *weights),
        [whole((64, 1536))] * 8 + [weight_spec] * 4,
        [jax.ShapeDtypeStruct((128, 1536), bf16)] * 4 + [jax.ShapeDtypeStruct((512, 1536), bf16)],
        [pl.BlockSpec((128, tile), lambda t, where: (0, t))] * 4 + [whole_out((512, 1536))],
        [],
    )
    return results[:4], results[4]


def join(chunks, joined):
    at = 0
    for chunk in chunks:
        joined[at : at + chunk.shape[0], :] = chunk[...]
        at += chunk.shape[0]


def spread(held, outs, q, y, step):
    for slot in range(8):
        row = pl.ds(pl.multiple_of(chunk_row(slot, y), 64), 64)
        for k in range(4):
            columns = pl.ds(pl.multiple_of(feature(q, k) + step * 128, 128), 128)
            outs[slot][:, columns] = held[row, k * 128 : (k + 1) * 128]


def branch_kernel(where, chunks, weights, cot):
    def kernel(where, *refs):
        chunks, weights, cot = refs[:5], refs[5:9], refs[9]
        outs, blocks, joined, held = refs[10:18], refs[18:22], refs[22], refs[23]
        q, y = where[0], where[1]
        step = pl.program_id(0)

        @pl.when(step == 0)
        def _():
            join(chunks, joined)

        side = jnp.concatenate([weights[k][...] for k in range(4)], axis=1)
        held[...] = jnp.dot(joined[...], side, preferred_element_type=f32).astype(bf16)
        spread(held, outs, q, y, step)
        units = pl.ds(pl.multiple_of(step * tile, tile), tile)
        product = transposed_dot(joined[:, units], cot[...]).astype(bf16)
        for at in range(4):
            blocks[at][...] = product[:, at * 384 : (at + 1) * 384]

    results = run_kernel(
        kernel,
        where,
        (*chunks, *weights, cot),
        [whole(chunk.shape) for chunk in chunks]
        + [pl.BlockSpec((1536, 128), lambda t, where: (0, t))] * 4
        + [whole((512, 1536))],
        [jax.ShapeDtypeStruct((2, 64, 1536), bf16)] * 8 + [jax.ShapeDtypeStruct((1536, 384), bf16)] * 4,
        [half_spec(0)] * 8 + [pl.BlockSpec((tile, 384), lambda t, where: (t, 0))] * 4,
        [pltpu.VMEM((512, 1536), bf16), pltpu.VMEM((512, tile), bf16)],
        products=2,
    )
    return results[:8], results[8:]


def carried_kernel(where, chunks, weights, pairs):
    def kernel(where, *refs):
        chunks, weights, outs, joined, held = refs[:5], refs[5:9], refs[17:25], refs[25], refs[26]
        q, y = where[0], where[1]
        step = pl.program_id(0)

        @pl.when(step == 0)
        def _():
            join(chunks, joined)

        side = jnp.concatenate([weights[k][...] for k in range(4)], axis=0)
        held[...] = lax.dot_general(
            joined[...], side, (((1,), (1,)), ((), ())), preferred_element_type=f32
        ).astype(bf16)
        spread(held, outs, q, y, step)

    results = run_kernel(
        kernel,
        where,
        (*chunks, *weights, *pairs),
        [whole(chunk.shape) for chunk in chunks]
        + [pl.BlockSpec((128, 1536), lambda t, where: (t, 0))] * 4
        + [pl.BlockSpec(memory_space=pl.ANY)] * 8,
        [jax.ShapeDtypeStruct((2, 64, 1536), bf16)] * 8 + [jax.ShapeDtypeStruct((512, 1536), bf16)],
        [half_spec(1)] * 8 + [whole_out((512, 1536))],
        [pltpu.VMEM((512, tile), bf16)],
        aliases={10 + slot: slot for slot in range(8)},
    )
    return results[:8], results[8]


def expand_kernel(where, upper, slopes):
    def kernel(where, upper, slopes, *blocks):
        step = pl.program_id(0)
        columns = [pl.ds(pl.multiple_of(at * 384 + step * 128, 128), 128) for at in range(4)]
        left = jnp.concatenate([upper[:, column] for column in columns], axis=1)
        product = transposed_dot(left, slopes[...]).astype(bf16)
        for at in range(4):
            blocks[at][...] = product[at * 128 : (at + 1) * 128]

    return run_kernel(
        kernel,
        where,
        (upper, slopes),
        [whole((512, 1536))] * 2,
        [jax.ShapeDtypeStruct((384, 1536), bf16)] * 4,
        [pl.BlockSpec((128, 1536), lambda t, where: (t, 0))] * 4,
        [],
    )


def body(upper_out, lower_out, upper_cot, lower_cot, w_expand, w_reduce):
    scale = 1.0 / math.sqrt(2048.0)
    q = 2 * lax.axis_index("xh") + lax.axis_index("core")
    where = jnp.stack([q, lax.axis_index("y"), lax.axis_index("z")]).astype(jnp.int32)

    start = enter(jnp.stack([upper_out, lower_cot]))
    start, w_expand, where = together(start, w_expand, where)
    expand_far = move(w_expand, ("xh",), (1,))
    expand_near = move(w_expand, ("core",), (1,))

    upper, cot = {0: start[0]}, {0: start[1]}
    upper[-1], upper[1], expand_near = together(z_move(upper[0], 1), z_move(upper[0], -1), expand_near)
    upper[-2], upper[2] = together(z_move(upper[-1], 1), z_move(upper[1], -1))
    upper[-3], upper[3], cot[-1], cot[1], expand_far, w_reduce = together(
        z_move(upper[-2], 1), z_move(upper[2], -1), z_move(cot[0], 1), z_move(cot[0], -1), expand_far, w_reduce
    )
    reduce_far = quad_move(w_reduce, 2)
    upper[4], expand_last, reduce_near, cot[-1], cot[1] = together(
        z_move(upper[-3], 1), quad_move(expand_far, 1), quad_move(w_reduce, 1), cot[-1], cot[1]
    )
    expand_all = [w_expand, expand_near, expand_far, expand_last]
    pre_parts, upper = part_kernel(where, [upper[offset] for offset in offsets], expand_all, 0)
    cot[-1], cot[1], *pre_parts = together(cot[-1], cot[1], *pre_parts)
    pre_one, pre_three, cot[-2], cot[2], pre_two = together(
        y_move(pre_parts[1], 1), y_move(pre_parts[3], 3), z_move(cot[-1], 1), z_move(cot[1], -1), pre_parts[2]
    )
    pre_two, cot[-3], cot[3], reduce_far = together(
        y_move(pre_two, 2), z_move(cot[-2], 1), z_move(cot[2], -1), reduce_far
    )
    pre = add(pre_parts[0], pre_one, pre_two, pre_three)
    act_own = jax.nn.gelu(pre, approximate=False).astype(bf16)

    act_own, reduce_far = together(act_own, reduce_far)
    last, following = y_move(act_own, 1), y_move(act_own, 3)
    cot[4], reduce_last = together(z_move(cot[-3], 1), quad_move(reduce_far, 1))
    reduce_all = [w_reduce, reduce_near, reduce_far, reduce_last]
    back_parts, cot = part_kernel(where, [cot[offset] for offset in offsets], reduce_all, 1)
    last, following, *back_parts = together(last, following, *back_parts)
    top, bottom, back_one, back_three, back_two = together(
        y_move(last[:64], 1), y_move(following[64:], 3), y_move(back_parts[1], 1), y_move(back_parts[3], 3), back_parts[2]
    )

    pairs, blocks = branch_kernel(where, [act_own, following, top, bottom, last], reduce_all, cot)
    back_two, *blocks = together(y_move(back_two, 2), *blocks)
    back = add(back_parts[0], back_one, back_two, back_three)
    slope_own = (back * gelu_slope(pre)).astype(bf16)

    slope_own, blocks[0], blocks[2] = together(slope_own, blocks[0], blocks[2])
    following, last, got_far, reduce_got = together(
        y_move(slope_own, 3), y_move(slope_own, 1), quad_move(blocks[0], 1), quad_move(blocks[2], 1)
    )
    far = [add(blocks[1][rows], got_far[rows]).astype(bf16) for rows in thirds(1536)]
    top, bottom, *far = together(last[:64], following[64:], *far)
    top, bottom, far[0] = together(y_move(top, 1), y_move(bottom, 3), quad_move(far[0], 2))

    pairs, slopes = carried_kernel(where, [slope_own, following, top, bottom, last], expand_all, pairs)
    part = dict(zip(offsets, pairs))

    ahead, behind, far[1] = together(part[4][0], part[4][1], far[1])
    ahead, behind, far[1], *more = together(
        z_move(ahead, 1), z_move(behind, -1), quad_move(far[1], 2), *expand_kernel(where, upper, slopes)
    )
    ahead = jnp.stack([add(ahead, part[3][0]).astype(bf16), part[3][1]])
    behind = jnp.stack([part[-3][0], add(behind, part[-3][1]).astype(bf16)])
    ahead, behind, far[2], more[0] = together(ahead, behind, far[2], more[0])
    ahead, behind, far[2], got_far = together(
        z_move(ahead, 1), z_move(behind, -1), quad_move(far[2], 2), quad_move(more[0], 1)
    )
    riders = [add(more[1][rows], got_far[rows]).astype(bf16) for rows in halves(384)]
    for step in (2, 1):
        ahead = add(ahead, part[step]).astype(bf16)
        behind = add(behind, part[-step]).astype(bf16)
        ahead, behind, riders[2 - step] = together(ahead, behind, riders[2 - step])
        inside = [quad_move(more[2], 1)] if step == 2 else []
        ahead, behind, riders[2 - step], *inside = together(
            z_move(ahead, 1), z_move(behind, -1), quad_move(riders[2 - step], 2), *inside
        )
        if step == 2:
            got = inside[0]
    left = leave(add(ahead, behind, part[0]).astype(bf16))
    lower_input = (lower_out.astype(f32) - left[0]).astype(bf16)
    upper_total = (upper_cot.astype(f32) + left[1]).astype(bf16)

    reduce_grad = jnp.concatenate(
        [
            (add(blocks[3][rows], reduce_got[rows], piece) * scale).astype(bf16)
            for rows, piece in zip(thirds(1536), far)
        ]
    )
    expand_grad = jnp.concatenate(
        [(add(more[3][rows], got[rows], piece) * scale).astype(bf16) for rows, piece in zip(halves(384), riders)]
    )
    return (lower_input, upper_total, expand_grad, reduce_grad)


def solution(mesh):
    fine = Mesh(mesh.devices.reshape(tuple(sizes[name] for name in axes)), axes)
    row, col = ("xl", "z"), ("y", "xh", "core")
    return jax.shard_map(
        body,
        mesh=fine,
        in_specs=(P(row, col), P(row, col), P(row, col), P(row, col), P(col, row), P(row, col)),
        out_specs=(P(row, col), P(row, col), P(col, row), P(row, col)),
        check_vma=False,
    )
```

```python
import math

import jax
import jax.numpy as jnp
import numpy as np
from jax import lax
from jax.experimental import pallas as pl
from jax.experimental.pallas import tpu as pltpu
from jax.sharding import Mesh, PartitionSpec as P

root_half = 0.7071067811865476
inv_root_tau = 0.3989422804014327
axes = ("xl", "z", "y", "xh", "core")
sizes = dict(xl=2, z=8, y=4, xh=2, core=2)
f32 = jnp.float32
bf16 = jnp.bfloat16
offsets = (0, -1, 1, -2, 2, -3, 3, 4)
flips = (3, 2, 1, 0)
tile = 512
narrow = 256


def gelu_slope(pre):
    return 0.5 * (1.0 + lax.erf(pre * root_half)) + pre * jnp.exp(-0.5 * pre * pre) * inv_root_tau


def move(value, names, steps):
    dims = tuple(sizes[name] for name in names)
    pairs = []
    for source in range(math.prod(dims)):
        at = np.unravel_index(source, dims)
        to = tuple((int(a) + s) % d for a, s, d in zip(at, steps, dims))
        pairs.append((source, int(np.ravel_multi_index(to, dims))))
    return lax.ppermute(value, names, pairs)


def together(*values):
    return lax.optimization_barrier(values)


def add(*values):
    return sum((value.astype(f32) for value in values[1:]), values[0].astype(f32))


def enter(values):
    n = values.shape[0]
    sent = jnp.broadcast_to(values.reshape(n, 1, 4, 32, 384).transpose(1, 2, 0, 3, 4), (2, 4, n, 32, 384))
    got = lax.all_to_all(sent.reshape(8, n, 32, 384), ("xl", "xh", "core"), 0, 0, tiled=True)
    return got.reshape(2, 4, n, 32, 384).transpose(2, 0, 3, 1, 4).reshape(n, 64, 1536)


def leave(rows):
    n = rows.shape[0]
    sent = rows.astype(bf16).reshape(n, 2, 32, 4, 384).transpose(1, 3, 0, 2, 4).reshape(8, n, 32, 384)
    got = lax.all_to_all(sent, ("xl", "xh", "core"), 0, 0, tiled=True)
    got = got.reshape(2, 4, n, 32, 384).astype(f32)
    return (got[0] + got[1]).transpose(1, 0, 2, 3).reshape(n, 128, 384)


def chunk_row(slot, y):
    return lax.rem(slot // 2 - y + 4, 4) * 128 + slot % 2 * 64


def feature(q, flip):
    return pl.multiple_of((q ^ flip) * 384, 128)


def y_move(value, k):
    return move(value, ("y",), (k,))


def quad_move(value, k):
    return move(value, ("xh", "core"), (k >> 1, k & 1))


def thirds(size):
    return [slice(at * size // 3, (at + 1) * size // 3) for at in range(3)]


def halves(size):
    return [slice(0, size // 2), slice(size // 2, size)]


def z_move(value, k):
    return move(value, ("z",), (k,))


def run_kernel(kernel, where, inputs, in_specs, outputs, out_specs, scratch, products=1, aliases=None, steps=3):
    spec = pltpu.PrefetchScalarGridSpec(
        num_scalar_prefetch=1, grid=(steps,), in_specs=in_specs, out_specs=out_specs, scratch_shapes=scratch
    )
    return pl.pallas_call(
        kernel,
        grid_spec=spec,
        out_shape=outputs,
        input_output_aliases=aliases or {},
        compiler_params=pltpu.CompilerParams(vmem_limit_bytes=(8 + 8 * products) << 20),
        cost_estimate=pl.CostEstimate(
            flops=products * 2 * 512 * 1536 * 1536, bytes_accessed=9 << 20, transcendentals=0
        ),
    )(where, *inputs)


def whole(shape):
    return pl.BlockSpec(shape, lambda t, where: (0,) * len(shape), pipeline_mode=pl.Buffered(1))


def whole_out(shape):
    return pl.BlockSpec(shape, lambda t, where: (0,) * len(shape))


def half_spec(which):
    return pl.BlockSpec((None, 64, 1536), lambda t, where: (which, 0, 0))


def transposed_dot(left, right):
    return lax.dot_general(left, right, (((0,), (0,)), ((), ())), preferred_element_type=f32)


def part_kernel(where, pieces, weights, which):
    def kernel(where, *refs):
        sources, weights, outs, ordered = refs[:8], refs[8:12], refs[12:16], refs[16]
        q, y = where[0], where[1]

        @pl.when(pl.program_id(0) == 0)
        def _():
            for slot in range(8):
                row = pl.ds(pl.multiple_of(chunk_row(slot, y), 64), 64)
                for at, flip in enumerate(flips):
                    columns = pl.ds(feature(q, flip), 384)
                    ordered[row, at * 384 : (at + 1) * 384] = sources[slot][:, columns]

        joined = jnp.concatenate([weights[k][...] for k in flips], axis=which)
        product = lax.dot_general(
            ordered[...], joined, (((1,), (which,)), ((), ())), preferred_element_type=f32
        ).astype(bf16)
        for k in range(4):
            outs[k][...] = product[k * 128 : (k + 1) * 128]

    if which:
        weight_spec = pl.BlockSpec((narrow, 384), lambda t, where: (t, 0))
    else:
        weight_spec = pl.BlockSpec((384, narrow), lambda t, where: (0, t))
    results = run_kernel(
        kernel,
        where,
        (*pieces, *weights),
        [whole((64, 1536))] * 8 + [weight_spec] * 4,
        [jax.ShapeDtypeStruct((128, 1536), bf16)] * 4 + [jax.ShapeDtypeStruct((512, 1536), bf16)],
        [pl.BlockSpec((128, narrow), lambda t, where: (0, t))] * 4 + [whole_out((512, 1536))],
        [],
        steps=6,
    )
    return results[:4], results[4]


def join(chunks, joined):
    at = 0
    for chunk in chunks:
        joined[at : at + chunk.shape[0], :] = chunk[...]
        at += chunk.shape[0]


def spread(held, outs, q, y, step):
    for slot in range(8):
        row = pl.ds(pl.multiple_of(chunk_row(slot, y), 64), 64)
        for k in range(4):
            columns = pl.ds(pl.multiple_of(feature(q, k) + step * 128, 128), 128)
            outs[slot][:, columns] = held[row, k * 128 : (k + 1) * 128]


def branch_kernel(where, chunks, weights, cot):
    def kernel(where, *refs):
        chunks, weights, cot = refs[:5], refs[5:9], refs[9]
        outs, blocks, joined, held = refs[10:18], refs[18:22], refs[22], refs[23]
        q, y = where[0], where[1]
        step = pl.program_id(0)

        @pl.when(step == 0)
        def _():
            join(chunks, joined)

        side = jnp.concatenate([weights[k][...] for k in range(4)], axis=1)
        held[...] = jnp.dot(joined[...], side, preferred_element_type=f32).astype(bf16)
        spread(held, outs, q, y, step)
        units = pl.ds(pl.multiple_of(step * tile, tile), tile)
        product = transposed_dot(joined[:, units], cot[...]).astype(bf16)
        for at in range(4):
            blocks[at][...] = product[:, at * 384 : (at + 1) * 384]

    results = run_kernel(
        kernel,
        where,
        (*chunks, *weights, cot),
        [whole(chunk.shape) for chunk in chunks]
        + [pl.BlockSpec((1536, 128), lambda t, where: (0, t))] * 4
        + [whole((512, 1536))],
        [jax.ShapeDtypeStruct((2, 64, 1536), bf16)] * 8 + [jax.ShapeDtypeStruct((1536, 384), bf16)] * 4,
        [half_spec(0)] * 8 + [pl.BlockSpec((tile, 384), lambda t, where: (t, 0))] * 4,
        [pltpu.VMEM((512, 1536), bf16), pltpu.VMEM((512, tile), bf16)],
        products=2,
    )
    return results[:8], results[8:]


def carried_kernel(where, chunks, weights, pairs):
    def kernel(where, *refs):
        chunks, weights, outs, joined, held = refs[:5], refs[5:9], refs[17:25], refs[25], refs[26]
        q, y = where[0], where[1]
        step = pl.program_id(0)

        @pl.when(step == 0)
        def _():
            join(chunks, joined)

        side = jnp.concatenate([weights[k][...] for k in range(4)], axis=0)
        held[...] = lax.dot_general(
            joined[...], side, (((1,), (1,)), ((), ())), preferred_element_type=f32
        ).astype(bf16)
        spread(held, outs, q, y, step)

    results = run_kernel(
        kernel,
        where,
        (*chunks, *weights, *pairs),
        [whole(chunk.shape) for chunk in chunks]
        + [pl.BlockSpec((128, 1536), lambda t, where: (t, 0))] * 4
        + [pl.BlockSpec(memory_space=pl.ANY)] * 8,
        [jax.ShapeDtypeStruct((2, 64, 1536), bf16)] * 8 + [jax.ShapeDtypeStruct((512, 1536), bf16)],
        [half_spec(1)] * 8 + [whole_out((512, 1536))],
        [pltpu.VMEM((512, tile), bf16)],
        aliases={10 + slot: slot for slot in range(8)},
    )
    return results[:8], results[8]


def expand_kernel(where, upper, slopes):
    def kernel(where, upper, slopes, *blocks):
        step = pl.program_id(0)
        columns = [pl.ds(pl.multiple_of(at * 384 + step * 128, 128), 128) for at in range(4)]
        left = jnp.concatenate([upper[:, column] for column in columns], axis=1)
        product = transposed_dot(left, slopes[...]).astype(bf16)
        for at in range(4):
            blocks[at][...] = product[at * 128 : (at + 1) * 128]

    return run_kernel(
        kernel,
        where,
        (upper, slopes),
        [whole((512, 1536))] * 2,
        [jax.ShapeDtypeStruct((384, 1536), bf16)] * 4,
        [pl.BlockSpec((128, 1536), lambda t, where: (t, 0))] * 4,
        [],
    )


def body(upper_out, lower_out, upper_cot, lower_cot, w_expand, w_reduce):
    scale = 1.0 / math.sqrt(2048.0)
    q = 2 * lax.axis_index("xh") + lax.axis_index("core")
    where = jnp.stack([q, lax.axis_index("y"), lax.axis_index("z")]).astype(jnp.int32)

    start = enter(jnp.stack([upper_out, lower_cot]))
    start, w_expand, where = together(start, w_expand, where)
    expand_far = move(w_expand, ("xh",), (1,))
    expand_near = move(w_expand, ("core",), (1,))

    upper, cot = {0: start[0]}, {0: start[1]}
    upper[-1], upper[1], expand_near = together(z_move(upper[0], 1), z_move(upper[0], -1), expand_near)
    upper[-2], upper[2] = together(z_move(upper[-1], 1), z_move(upper[1], -1))
    upper[-3], upper[3], cot[-1], cot[1], expand_far, w_reduce = together(
        z_move(upper[-2], 1), z_move(upper[2], -1), z_move(cot[0], 1), z_move(cot[0], -1), expand_far, w_reduce
    )
    reduce_far = quad_move(w_reduce, 2)
    upper[4], expand_last, reduce_near, cot[-1], cot[1] = together(
        z_move(upper[-3], 1), quad_move(expand_far, 1), quad_move(w_reduce, 1), cot[-1], cot[1]
    )
    expand_all = [w_expand, expand_near, expand_far, expand_last]
    pre_parts, upper = part_kernel(where, [upper[offset] for offset in offsets], expand_all, 0)
    cot[-1], cot[1], *pre_parts = together(cot[-1], cot[1], *pre_parts)
    pre_one, pre_three, cot[-2], cot[2], pre_two = together(
        y_move(pre_parts[1], 1), y_move(pre_parts[3], 3), z_move(cot[-1], 1), z_move(cot[1], -1), pre_parts[2]
    )
    pre_two, cot[-3], cot[3], reduce_far = together(
        y_move(pre_two, 2), z_move(cot[-2], 1), z_move(cot[2], -1), reduce_far
    )
    pre = add(pre_parts[0], pre_one, pre_two, pre_three)
    act_own = jax.nn.gelu(pre, approximate=False).astype(bf16)

    act_own, reduce_far = together(act_own, reduce_far)
    last, following = y_move(act_own, 1), y_move(act_own, 3)
    cot[4], reduce_last = together(z_move(cot[-3], 1), quad_move(reduce_far, 1))
    reduce_all = [w_reduce, reduce_near, reduce_far, reduce_last]
    back_parts, cot = part_kernel(where, [cot[offset] for offset in offsets], reduce_all, 1)
    last, following, *back_parts = together(last, following, *back_parts)
    top, bottom, back_one, back_three, back_two = together(
        y_move(last[:64], 1), y_move(following[64:], 3), y_move(back_parts[1], 1), y_move(back_parts[3], 3), back_parts[2]
    )

    pairs, blocks = branch_kernel(where, [act_own, following, top, bottom, last], reduce_all, cot)
    back_two, *blocks = together(y_move(back_two, 2), *blocks)
    back = add(back_parts[0], back_one, back_two, back_three)
    slope_own = (back * gelu_slope(pre)).astype(bf16)

    slope_own, blocks[0], blocks[2] = together(slope_own, blocks[0], blocks[2])
    following, last, got_far, reduce_got = together(
        y_move(slope_own, 3), y_move(slope_own, 1), quad_move(blocks[0], 1), quad_move(blocks[2], 1)
    )
    far = [add(blocks[1][rows], got_far[rows]).astype(bf16) for rows in thirds(1536)]
    top, bottom, *far = together(last[:64], following[64:], *far)
    top, bottom, far[0] = together(y_move(top, 1), y_move(bottom, 3), quad_move(far[0], 2))

    pairs, slopes = carried_kernel(where, [slope_own, following, top, bottom, last], expand_all, pairs)
    part = dict(zip(offsets, pairs))

    ahead, behind, far[1] = together(part[4][0], part[4][1], far[1])
    ahead, behind, far[1], *more = together(
        z_move(ahead, 1), z_move(behind, -1), quad_move(far[1], 2), *expand_kernel(where, upper, slopes)
    )
    ahead = jnp.stack([add(ahead, part[3][0]).astype(bf16), part[3][1]])
    behind = jnp.stack([part[-3][0], add(behind, part[-3][1]).astype(bf16)])
    ahead, behind, far[2], more[0] = together(ahead, behind, far[2], more[0])
    ahead, behind, far[2], got_far = together(
        z_move(ahead, 1), z_move(behind, -1), quad_move(far[2], 2), quad_move(more[0], 1)
    )
    riders = [add(more[1][rows], got_far[rows]).astype(bf16) for rows in halves(384)]
    for step in (2, 1):
        ahead = add(ahead, part[step]).astype(bf16)
        behind = add(behind, part[-step]).astype(bf16)
        ahead, behind, riders[2 - step] = together(ahead, behind, riders[2 - step])
        inside = [quad_move(more[2], 1)] if step == 2 else []
        ahead, behind, riders[2 - step], *inside = together(
            z_move(ahead, 1), z_move(behind, -1), quad_move(riders[2 - step], 2), *inside
        )
        if step == 2:
            got = inside[0]
    left = leave(add(ahead, behind, part[0]).astype(bf16))
    lower_input = (lower_out.astype(f32) - left[0]).astype(bf16)
    upper_total = (upper_cot.astype(f32) + left[1]).astype(bf16)

    reduce_grad = jnp.concatenate(
        [
            (add(blocks[3][rows], reduce_got[rows], piece) * scale).astype(bf16)
            for rows, piece in zip(thirds(1536), far)
        ]
    )
    expand_grad = jnp.concatenate(
        [(add(more[3][rows], got[rows], piece) * scale).astype(bf16) for rows, piece in zip(halves(384), riders)]
    )
    return (lower_input, upper_total, expand_grad, reduce_grad)


def solution(mesh):
    fine = Mesh(mesh.devices.reshape(tuple(sizes[name] for name in axes)), axes)
    row, col = ("xl", "z"), ("y", "xh", "core")
    return jax.shard_map(
        body,
        mesh=fine,
        in_specs=(P(row, col), P(row, col), P(row, col), P(row, col), P(col, row), P(row, col)),
        out_specs=(P(row, col), P(row, col), P(col, row), P(row, col)),
        check_vma=False,
    )
```
